512 devices in a mesh: expert: 128 (over z, y, core), dp: 4 (over x).
Axes of the slice: x: 4, y: 8, z: 8, core: 2. Of those that a mesh axis runs over, the one named last changes fastest.
Arguments:
- tokens: bfloat16 [256, 4096], P('expert', 'dp'), may hold values from -6 to 6
- routing: int32 [256, 8], P('expert'), may hold values from 0 to 31, all different within a row; in each aligned block of 2 rows (0 to 1, 2 to 3, ...) at most 2 rows name the same one
- combine_weights: float32 [256, 8], P('expert'), may hold values from 0.05 to 0.4
- gate_weight: bfloat16 [49152, 4096], P('expert', 'dp'), may hold values from -0.09375 to 0.09375
- up_weight: bfloat16 [49152, 4096], P('expert', 'dp'), may hold values from -0.09375 to 0.09375
- down_weight: bfloat16 [49152, 4096], P('expert', 'dp'), may hold values from -0.15625 to 0.15625
Outputs:
- layer_output: bfloat16 [256, 4096], P('expert', 'dp')
The draws below stay inside these ranges and needn't reach their ends.
Inputs may be any that keep to these rules, and one draw needn't show every extreme that they name: `routing`: each row names 8 different experts. Among the 2 rows of one index of the expert axis, no expert is named by more than 2 rows, and in some of these blocks one expert is named by exactly 2.
All inputs are finite; a program needn't handle non-finite values.
Results may differ from the reference program's by a relative error of at most 0.025.
Values may be sent and summed in bfloat16 or wider, within the bound.
A program may use at most 64 MiB of HBM per device.

```python
import math
import jax
import jax.numpy as jnp
import numpy as np
from jax import lax

D = 4096
FF = 1536
TOK_DEV = 2
EXPERTS = 32
SLICES = 4
TOPK = 8
CAP = 2
TOKENS = 256
N_DP = 4


def level_of(key, shape, cuts, least, high):
    gain, own = 1.0, jax.random.fold_in(key, 6)
    for dim, parts in cuts:
        heights = jnp.exp(jax.random.uniform(jax.random.fold_in(own, dim), (parts,), jnp.float32, least / len(cuts), high / len(cuts)))
        gain = gain * jnp.repeat(heights, shape[dim] // parts).reshape([-1 if axis == dim else 1 for axis in range(len(shape))])
    return gain


def assign_block(stream_key, own, number, rows, number_of, top, most, lean):
    ranking = jax.random.permutation(stream_key, number_of)
    packed, common = load_shares(number_of, rows * top, most, lean, True), load_shares(number_of, rows * top, most, lean, False)
    places = jnp.arange(number_of)

    def named(tallies, turn):
        used = int((tallies > 0).sum())
        fixed = max(1, used // 4)
        shifted = fixed + (places - fixed + turn * (used - fixed)) % max(1, number_of - fixed)
        return jnp.zeros((number_of,), jnp.int32).at[ranking[jnp.where(places < fixed, places, shifted)]].set(jnp.asarray(tallies, jnp.int32))

    tallies = jnp.where(number % 4 == 0, named(packed, number // 4), named(common, number - number // 4 - 1))
    mixed = jax.random.permutation(jax.random.fold_in(own, 3), number_of)
    source_of, receiver = mixed[0:number_of // 2 * 2:2], mixed[1:number_of // 2 * 2:2]
    room = jnp.minimum(tallies[source_of] - 1, most - tallies[receiver]) // 2
    room = jnp.where((source_of == ranking[0]) | (receiver == ranking[0]) | (tallies[receiver] == 0), 0, jnp.maximum(room, 0))
    shifted = jax.random.randint(jax.random.fold_in(own, 4), (number_of // 2,), 0, 1 << 20) % (room + 1)
    tallies = tallies.at[source_of].add(-shifted).at[receiver].add(shifted)
    labels = jnp.searchsorted(jnp.cumsum(tallies), jnp.arange(rows * top), side="right").astype(jnp.int32)
    table = labels.reshape(top, rows).T
    table = table[jax.random.permutation(jax.random.fold_in(own, 1), rows)]
    turn = jax.random.randint(jax.random.fold_in(own, 2), (rows, 1), 0, top)
    return jnp.take_along_axis(table, (jnp.arange(top)[None, :] + turn) % top, axis=1)


def load_shares(count, total, reach, lean, full):
    weights = [(1 << 20) // math.isqrt(grade ** lean) + 1 for grade in range(1, count + 1)]
    largest = reach if full else min(reach, max(-(-total // count), total * weights[0] // sum(weights)))
    least = 1 if total - largest >= count - 1 else 0
    counts, spare = [largest] + [least] * (count - 1), total - largest - least * (count - 1)
    while spare > 0:
        candidates = [i for i in range(1, count) if counts[i] < largest] or [i for i in range(1, count) if counts[i] < reach]
        pool, remaining = sum([weights[i] for i in candidates]), spare
        for i in candidates:
            extra = min(reach - counts[i], max(1, remaining * weights[i] // pool), spare)
            counts[i] = counts[i] + extra
            spare = spare - extra
    return np.array(counts)


def scatter_about(key, dims, scale, bound, pieces=(), held_as=jnp.bfloat16):
    factor_of = level_of(key, dims, pieces, -0.22, 0.18) if pieces else 1.0
    array = jax.random.normal(key, dims, jnp.float32) * scale * factor_of
    return jnp.minimum(jnp.maximum(array, -bound), bound).astype(held_as)


def setup_inputs(seed: int = 0) -> dict:
    key_list = jax.random.split(jax.random.key(seed), 7)
    tokens = scatter_about(key_list[0], (TOKENS, D), 1.0, 6.0, ((0, 128), (1, 4)))
    routing_keys = jax.random.split(jax.random.fold_in(key_list[1], 1), TOKENS // TOK_DEV)
    routing_turns = jax.random.permutation(jax.random.fold_in(key_list[1], 3), TOKENS // TOK_DEV)
    routing = jax.vmap(lambda own, number: assign_block(jax.random.fold_in(key_list[1], 2), own, number, TOK_DEV, EXPERTS, TOPK, CAP, 2))(routing_keys, routing_turns).reshape((TOKENS, TOPK))
    combine_weights = jnp.clip(jnp.exp(math.log(0.4) - 2.0794415 * jax.random.uniform(key_list[2], (TOKENS, TOPK), jnp.float32) ** level_of(key_list[2], (TOKENS, TOPK), ((0, 128),), -0.2, 0.2)), 0.05, 0.4)
    gate_weight = scatter_about(key_list[3], (EXPERTS * FF, D), D ** -0.5, 0.09375, ((0, 128), (1, 4)))
    up_weight = scatter_about(key_list[4], (EXPERTS * FF, D), D ** -0.5, 0.09375, ((0, 128), (1, 4)))
    down_weight = scatter_about(key_list[5], (EXPERTS * FF, D), FF ** -0.5, 0.15625, ((0, 128), (1, 4)))
    return dict(tokens=tokens, routing=routing, combine_weights=combine_weights, gate_weight=gate_weight, up_weight=up_weight, down_weight=down_weight)


highest = lax.Precision.HIGHEST


def rounded(values):
    return lax.optimization_barrier(values.astype(jnp.bfloat16)).astype(jnp.float32)


def quarter_sum(left_side, right_side):
    quarter = D // N_DP
    left_parts = left_side.reshape(left_side.shape[0], N_DP, quarter)
    right_parts = right_side.reshape(right_side.shape[0], N_DP, quarter)
    partials = jnp.einsum("tqd,fqd->tqf", left_parts, right_parts, precision=highest)
    return jnp.sum(rounded(partials), axis=1)


def slice_sum(left_side, right_side):
    left_parts = left_side.reshape(left_side.shape[0], SLICES, FF // SLICES)
    right_parts = right_side.reshape(SLICES, FF // SLICES, right_side.shape[1])
    product = jnp.einsum("tsf,sfd->tsd", left_parts, right_parts, precision=highest)
    return jnp.sum(rounded(product), axis=1)


def reference(tokens, routing, combine_weights, gate_weight, up_weight, down_weight):
    token_values = tokens.astype(jnp.float32)
    gate_all = gate_weight.reshape(EXPERTS, FF, D)
    up_all = up_weight.reshape(EXPERTS, FF, D)
    down_all = down_weight.reshape(EXPERTS, FF, D)

    def per_expert(output_sum, inputs):
        expert, gate_rows, up_rows, down_rows = inputs
        gate_rows = gate_rows.astype(jnp.float32)
        up_rows = up_rows.astype(jnp.float32)
        down_rows = down_rows.astype(jnp.float32)
        picked = routing == expert
        weight = jnp.sum(jnp.where(picked, combine_weights, jnp.zeros_like(combine_weights)), axis=1)
        chosen = jnp.any(picked, axis=1)
        sent_rows = jnp.where(chosen[:, None], token_values, jnp.zeros_like(token_values))
        pre_gate = quarter_sum(sent_rows, gate_rows)
        pre_up = quarter_sum(sent_rows, up_rows)
        hidden = rounded(jax.nn.sigmoid(pre_gate) * pre_gate * pre_up)
        output_sum = output_sum + weight[:, None] * slice_sum(hidden, down_rows)
        return output_sum, None

    start = jnp.zeros((TOKENS, D), jnp.float32)
    inputs = (jnp.arange(EXPERTS, dtype=jnp.int32), gate_all, up_all, down_all)
    output_sum, unused = lax.scan(per_expert, start, inputs)
    return output_sum.astype(jnp.bfloat16)
```

```python
import jax
import jax.numpy as jnp
from jax import lax
from jax.experimental import pallas as pl
from jax.experimental.pallas import tpu as pltpu
from jax.sharding import PartitionSpec as P

MESH = pl.DeviceIdType.MESH
F32, BF16 = jnp.float32, jnp.bfloat16
LINE = 8
FAR = (4, 3, 5, 2, 6, 1, 7)
NEAR = (1, 7, 2, 6, 3, 5, 4)
DP = (2, 1, 3)
D, H, PAY = 1024, 384, 1152
TOK, BLK = 2, 16
SLICES = 4
EXPERTS = 32


def body(tokens, routing, combine, gate_hbm, up_hbm, down_hbm, out,
         gate, up, down, pay, rows1, stage, gath, part, rs, hid, own, away, other, red, rows2, tmp,
         wsem, s1, r1, s2, r2, s3, r3, s4, r4, s5, r5, s6, r6, s7, r7, s8, r8):
    me = lax.axis_index("expert")
    x = lax.axis_index("dp")
    c = lax.rem(me, 2)
    y = lax.rem(me // 2, LINE)
    z = me // (2 * LINE)
    e = me // SLICES

    def at(a, b):
        zz = lax.rem(z + a * (1 - c) + b * c, LINE)
        yy = lax.rem(y + a * c + b * (1 - c), LINE)
        return ((zz * LINE + yy) * 2 + c, x)

    partner = (me + 1 - 2 * c, x)

    def over(d):
        return (me, lax.rem(x + d, 4))

    def send(src, dst, ssem, rsem, to):
        cp = pltpu.make_async_remote_copy(
            src_ref=src, dst_ref=dst, send_sem=ssem, recv_sem=rsem, device_id=to, device_id_type=MESH)
        cp.start()
        return cp

    barrier = pltpu.get_barrier_semaphore()
    for d in FAR:
        pl.semaphore_signal(barrier, inc=1, device_id=at(d, 0), device_id_type=MESH)
        pl.semaphore_signal(barrier, inc=1, device_id=at(0, d), device_id_type=MESH)
    for d in DP:
        pl.semaphore_signal(barrier, inc=1, device_id=over(d), device_id_type=MESH)
    pl.semaphore_signal(barrier, inc=1, device_id=partner, device_id_type=MESH)

    loads = [pltpu.make_async_copy(src, dst, wsem.at[i])
             for i, (src, dst) in enumerate(((gate_hbm, gate), (up_hbm, up), (down_hbm, down)))]
    for cp in loads:
        cp.start()

    pay[:, :D] = tokens[...]
    lane = lax.broadcasted_iota(jnp.int32, (TOK, 128), 1)
    dense = jnp.zeros((TOK, 128), F32)
    for k in range(8):
        dense = dense + jnp.where(lax.rem(lane, EXPERTS) == routing[:, k:k + 1], combine[:, k:k + 1], 0.0)
    high = dense.astype(BF16).astype(F32)
    pay[:, D:] = jnp.where(lane < EXPERTS, high, jnp.where(lane < 2 * EXPERTS, dense - high, 0.0)).astype(BF16)
    pl.semaphore_wait(barrier, 18)

    c1 = {d: send(pay, rows1.at[d], s1.at[d], r1.at[d], at(d, 0)) for d in FAR}
    stage[0:TOK, :] = pay[...].astype(F32)
    for d in NEAR:
        c1[d].wait_recv()
        stage[TOK * d:TOK * d + TOK, :] = rows1[d].astype(F32)
    gath[0, 0] = stage[...].astype(BF16)

    c2 = {d: send(gath.at[0, 0], gath.at[0, d], s2.at[d], r2.at[d], at(0, d)) for d in FAR}
    c3 = {0: send(gath.at[0, 0], gath.at[1, 0], s3.at[0], r3.at[0], partner)}
    for d in NEAR:
        c2[d].wait_recv()
        c3[d] = send(gath.at[0, d], gath.at[1, d], s3.at[d], r3.at[d], partner)
    for cp in loads:
        cp.wait()

    def linear(h):
        rows = gath[h, :, :, :D].reshape(128, D)
        for i, w in enumerate((gate, up)):
            lin = lax.dot_general(rows, w[...], (((1,), (1,)), ((), ())), preferred_element_type=F32)
            part[h, :, :, i * H:(i + 1) * H] = lin.astype(BF16).reshape(4, 32, H)
        return {d: send(part.at[h, lax.rem(x + d, 4)], rs.at[h, d], s4.at[h, d], r4.at[h, d], over(d)) for d in DP}

    c4 = [linear(0)]
    for d in range(LINE):
        c3[d].wait_recv()
    c4.append(linear(1))

    lanes = lax.broadcasted_iota(jnp.int32, (32, 128), 1)
    mine = (lanes == e) | (lanes == e + EXPERTS)

    def activate(h):
        total = part[h, x].astype(F32)
        for d in (1, 3, 2):
            c4[h][d].wait_recv()
            total = total + rs[h, d].astype(F32)
        wrow = gath[h, pl.ds(2 * x, 2), :, D:].reshape(32, 128).astype(F32)
        weight = jnp.sum(jnp.where(mine, wrow, 0.0), axis=1, keepdims=True)
        g, u = total[:, :H], total[:, H:]
        hid[h, x] = (jax.nn.sigmoid(g) * g * u * weight).astype(BF16)
        return {d: send(hid.at[h, x], hid.at[h, x], s5.at[h, d], r5.at[h, d], over(d)) for d in DP}

    c5 = [activate(0), activate(1)]

    def product(h):
        for d in (1, 3, 2):
            c5[h][d].wait_recv()
        return jnp.dot(hid[h].reshape(128, H), down[...], preferred_element_type=F32)

    own[...] = product(0).reshape(LINE, BLK, D)
    away[...] = product(1).astype(BF16).reshape(LINE, BLK, D)

    order = FAR + (0,)
    c6 = {d: send(away.at[d], other.at[d], s6.at[d], r6.at[d], partner) for d in order}
    c7 = {}
    for d in order:
        c6[d].wait_recv()
        own[d] = own[d] + other[d].astype(F32)
        if d:
            tmp[d] = own[d].astype(BF16)
            c7[d] = send(tmp.at[d], red.at[d], s7.at[d], r7.at[d], at(0, LINE - d))
    total = own[0]
    for d in NEAR:
        c7[d].wait_recv()
        total = total + red[d].astype(F32)
    own[0] = total
    c8 = {}
    for d in FAR:
        rows2[0, d] = own[0, TOK * d:TOK * d + TOK, :].astype(BF16)
        c8[d] = send(rows2.at[0, d], rows2.at[1, d], s8.at[d], r8.at[d], at(LINE - d, 0))
    final = own[0, 0:TOK, :]
    for d in NEAR:
        c8[d].wait_recv()
        final = final + rows2[1, d].astype(F32)
    out[...] = final.astype(BF16)

    for group in (c1, c2, c3, c4[0], c4[1], c5[0], c5[1], c6, c7, c8):
        for cp in group.values():
            cp.wait_send()


def shards(tokens, routing, combine, gate, up, down):
    vmem = pl.BlockSpec(memory_space=pltpu.VMEM)
    hbm = pl.BlockSpec(memory_space=pl.ANY)
    dma = pltpu.SemaphoreType.DMA
    return pl.pallas_call(
        body,
        out_shape=jax.ShapeDtypeStruct((TOK, D), BF16),
        in_specs=[vmem, vmem, vmem, hbm, hbm, hbm],
        out_specs=vmem,
        scratch_shapes=[
            pltpu.VMEM((H, D), BF16), pltpu.VMEM((H, D), BF16), pltpu.VMEM((H, D), BF16),
            pltpu.VMEM((TOK, PAY), BF16),
            pltpu.VMEM((LINE, TOK, PAY), BF16),
            pltpu.VMEM((BLK, PAY), F32),
            pltpu.VMEM((2, LINE, BLK, PAY), BF16),
            pltpu.VMEM((2, 4, 32, 2 * H), BF16),
            pltpu.VMEM((2, 4, 32, 2 * H), BF16),
            pltpu.VMEM((2, 4, 32, H), BF16),
            pltpu.VMEM((LINE, BLK, D), F32),
            pltpu.VMEM((LINE, BLK, D), BF16),
            pltpu.VMEM((LINE, BLK, D), BF16),
            pltpu.VMEM((LINE, BLK, D), BF16),
            pltpu.VMEM((2, LINE, TOK, D), BF16),
            pltpu.VMEM((LINE, BLK, D), BF16),
            dma((3,)),
            dma((8,)), dma((8,)), dma((8,)), dma((8,)), dma((8,)), dma((8,)),
            dma((2, 4)), dma((2, 4)), dma((2, 4)), dma((2, 4)),
            dma((8,)), dma((8,)), dma((8,)), dma((8,)), dma((8,)), dma((8,)),
        ],
        compiler_params=pltpu.CompilerParams(
            collective_id=0, has_side_effects=True, vmem_limit_bytes=48 << 20),
        cost_estimate=pl.CostEstimate(flops=603979776, bytes_accessed=2400000, transcendentals=24576),
    )(tokens, routing, combine, gate, up, down)


def solution(mesh):
    return jax.shard_map(
        shards,
        mesh=mesh,
        in_specs=(
            P("expert", "dp"),
            P("expert", None),
            P("expert", None),
            P("expert", "dp"),
            P("expert", "dp"),
            P("expert", "dp"),
        ),
        out_specs=P("expert", "dp"),
        check_vma=False,
    )
```

```python
import jax
import jax.numpy as jnp
from jax import lax
from jax.experimental import pallas as pl
from jax.experimental.pallas import tpu as pltpu
from jax.sharding import PartitionSpec as P

MESH = pl.DeviceIdType.MESH
F32, BF16 = jnp.float32, jnp.bfloat16
LINE = 8
FAR = (4, 3, 5, 2, 6, 1, 7)
NEAR = (1, 7, 2, 6, 3, 5, 4)
DP = (2, 1, 3)
D, H, PAY = 1024, 384, 1152
TOK, BLK = 2, 16
SLICES = 4
EXPERTS = 32


def body(tokens_hbm, routing_hbm, combine_hbm, gate_hbm, up_hbm, down_hbm, out,
         tokens, routing, combine, gate, up, down, pay, rows1, stage, gath, part, rs, hid, own, away, other, red, rows2, tmp,
         wsem, s1, r1, s2, r2, s3, r3, s4, r4, s5, r5, s6, r6, s7, r7, s8, r8):
    me = lax.axis_index("expert")
    x = lax.axis_index("dp")
    c = lax.rem(me, 2)
    y = lax.rem(me // 2, LINE)
    z = me // (2 * LINE)
    e = me // SLICES

    def at(a, b):
        zz = lax.rem(z + a * (1 - c) + b * c, LINE)
        yy = lax.rem(y + a * c + b * (1 - c), LINE)
        return ((zz * LINE + yy) * 2 + c, x)

    partner = (me + 1 - 2 * c, x)

    def over(d):
        return (me, lax.rem(x + d, 4))

    def send(src, dst, ssem, rsem, to):
        cp = pltpu.make_async_remote_copy(
            src_ref=src, dst_ref=dst, send_sem=ssem, recv_sem=rsem, device_id=to, device_id_type=MESH)
        cp.start()
        return cp

    barrier = pltpu.get_barrier_semaphore()
    for d in FAR:
        pl.semaphore_signal(barrier, inc=1, device_id=at(d, 0), device_id_type=MESH)
        pl.semaphore_signal(barrier, inc=1, device_id=at(0, d), device_id_type=MESH)
    for d in DP:
        pl.semaphore_signal(barrier, inc=1, device_id=over(d), device_id_type=MESH)
    pl.semaphore_signal(barrier, inc=1, device_id=partner, device_id_type=MESH)

    loads = [pltpu.make_async_copy(src, dst, wsem.at[i]) for i, (src, dst) in enumerate((
        (tokens_hbm, tokens), (routing_hbm, routing), (combine_hbm, combine),
        (gate_hbm, gate), (up_hbm, up), (down_hbm, down)))]
    for cp in loads:
        cp.start()
    for cp in loads[:3]:
        cp.wait()

    pay[:, :D] = tokens[...]
    lane = lax.broadcasted_iota(jnp.int32, (TOK, 128), 1)
    dense = jnp.zeros((TOK, 128), F32)
    for k in range(8):
        dense = dense + jnp.where(lax.rem(lane, EXPERTS) == routing[:, k:k + 1], combine[:, k:k + 1], 0.0)
    high = dense.astype(BF16).astype(F32)
    pay[:, D:] = jnp.where(lane < EXPERTS, high, jnp.where(lane < 2 * EXPERTS, dense - high, 0.0)).astype(BF16)
    pl.semaphore_wait(barrier, 18)

    c1 = {d: send(pay, rows1.at[d], s1.at[d], r1.at[d], at(d, 0)) for d in FAR}
    stage[0:TOK, :] = pay[...].astype(F32)
    for d in NEAR:
        c1[d].wait_recv()
        stage[TOK * d:TOK * d + TOK, :] = rows1[d].astype(F32)
    gath[0, 0] = stage[...].astype(BF16)

    c2 = {d: send(gath.at[0, 0], gath.at[0, d], s2.at[d], r2.at[d], at(0, d)) for d in FAR}
    c3 = {0: send(gath.at[0, 0], gath.at[1, 0], s3.at[0], r3.at[0], partner)}
    for d in NEAR:
        c2[d].wait_recv()
        c3[d] = send(gath.at[0, d], gath.at[1, d], s3.at[d], r3.at[d], partner)
    for cp in loads[3:]:
        cp.wait()

    def linear(h):
        rows = gath[h, :, :, :D].reshape(128, D)
        for i, w in enumerate((gate, up)):
            lin = lax.dot_general(rows, w[...], (((1,), (1,)), ((), ())), preferred_element_type=F32)
            part[h, :, :, i * H:(i + 1) * H] = lin.astype(BF16).reshape(4, 32, H)
        return {d: send(part.at[h, lax.rem(x + d, 4)], rs.at[h, d], s4.at[h, d], r4.at[h, d], over(d)) for d in DP}

    c4 = [linear(0)]
    for d in range(LINE):
        c3[d].wait_recv()
    c4.append(linear(1))

    lanes = lax.broadcasted_iota(jnp.int32, (32, 128), 1)
    mine = (lanes == e) | (lanes == e + EXPERTS)

    def activate(h):
        total = part[h, x].astype(F32)
        for d in (1, 3, 2):
            c4[h][d].wait_recv()
            total = total + rs[h, d].astype(F32)
        wrow = gath[h, pl.ds(2 * x, 2), :, D:].reshape(32, 128).astype(F32)
        weight = jnp.sum(jnp.where(mine, wrow, 0.0), axis=1, keepdims=True)
        g, u = total[:, :H], total[:, H:]
        hid[h, x] = (jax.nn.sigmoid(g) * g * u * weight).astype(BF16)
        return {d: send(hid.at[h, x], hid.at[h, x], s5.at[h, d], r5.at[h, d], over(d)) for d in DP}

    c5 = [activate(0), activate(1)]

    def product(h):
        for d in (1, 3, 2):
            c5[h][d].wait_recv()
        return jnp.dot(hid[h].reshape(128, H), down[...], preferred_element_type=F32)

    own[...] = product(0).reshape(LINE, BLK, D)
    away[...] = product(1).astype(BF16).reshape(LINE, BLK, D)

    order = FAR + (0,)
    c6 = {d: send(away.at[d], other.at[d], s6.at[d], r6.at[d], partner) for d in order}
    c7 = {}
    for d in order:
        c6[d].wait_recv()
        own[d] = own[d] + other[d].astype(F32)
        if d:
            tmp[d] = own[d].astype(BF16)
            c7[d] = send(tmp.at[d], red.at[d], s7.at[d], r7.at[d], at(0, LINE - d))
    total = own[0]
    for d in NEAR:
        c7[d].wait_recv()
        total = total + red[d].astype(F32)
    own[0] = total
    c8 = {}
    for d in FAR:
        rows2[0, d] = own[0, TOK * d:TOK * d + TOK, :].astype(BF16)
        c8[d] = send(rows2.at[0, d], rows2.at[1, d], s8.at[d], r8.at[d], at(LINE - d, 0))
    final = own[0, 0:TOK, :]
    for d in NEAR:
        c8[d].wait_recv()
        final = final + rows2[1, d].astype(F32)
    out[...] = final.astype(BF16)

    for group in (c1, c2, c3, c4[0], c4[1], c5[0], c5[1], c6, c7, c8):
        for cp in group.values():
            cp.wait_send()


def shards(tokens, routing, combine, gate, up, down):
    vmem = pl.BlockSpec(memory_space=pltpu.VMEM)
    hbm = pl.BlockSpec(memory_space=pl.ANY)
    dma = pltpu.SemaphoreType.DMA
    return pl.pallas_call(
        body,
        out_shape=jax.ShapeDtypeStruct((TOK, D), BF16),
        in_specs=[hbm] * 6,
        out_specs=vmem,
        scratch_shapes=[
            pltpu.VMEM((TOK, D), BF16), pltpu.VMEM((TOK, 8), jnp.int32), pltpu.VMEM((TOK, 8), F32),
            pltpu.VMEM((H, D), BF16), pltpu.VMEM((H, D), BF16), pltpu.VMEM((H, D), BF16),
            pltpu.VMEM((TOK, PAY), BF16),
            pltpu.VMEM((LINE, TOK, PAY), BF16),
            pltpu.VMEM((BLK, PAY), F32),
            pltpu.VMEM((2, LINE, BLK, PAY), BF16),
            pltpu.VMEM((2, 4, 32, 2 * H), BF16),
            pltpu.VMEM((2, 4, 32, 2 * H), BF16),
            pltpu.VMEM((2, 4, 32, H), BF16),
            pltpu.VMEM((LINE, BLK, D), F32),
            pltpu.VMEM((LINE, BLK, D), BF16),
            pltpu.VMEM((LINE, BLK, D), BF16),
            pltpu.VMEM((LINE, BLK, D), BF16),
            pltpu.VMEM((2, LINE, TOK, D), BF16),
            pltpu.VMEM((LINE, BLK, D), BF16),
            dma((6,)),
            dma((8,)), dma((8,)), dma((8,)), dma((8,)), dma((8,)), dma((8,)),
            dma((2, 4)), dma((2, 4)), dma((2, 4)), dma((2, 4)),
            dma((8,)), dma((8,)), dma((8,)), dma((8,)), dma((8,)), dma((8,)),
        ],
        compiler_params=pltpu.CompilerParams(
            collective_id=0, has_side_effects=True, vmem_limit_bytes=60 << 20),
        cost_estimate=pl.CostEstimate(flops=603979776, bytes_accessed=2400000, transcendentals=24576),
    )(tokens, routing, combine, gate, up, down)


def solution(mesh):
    return jax.shard_map(
        shards,
        mesh=mesh,
        in_specs=(
            P("expert", "dp"),
            P("expert", None),
            P("expert", None),
            P("expert", "dp"),
            P("expert", "dp"),
            P("expert", "dp"),
        ),
        out_specs=P("expert", "dp"),
        check_vma=False,
    )
```

```python
import jax
import jax.numpy as jnp
from jax import lax
from jax.experimental import pallas as pl
from jax.experimental.pallas import tpu as pltpu
from jax.sharding import PartitionSpec as P

MESH = pl.DeviceIdType.MESH
F32, BF16 = jnp.float32, jnp.bfloat16
LINE = 8
FAR = (4, 3, 5, 2, 6, 1, 7)
NEAR = (1, 7, 2, 6, 3, 5, 4)
DP = (2, 1, 3)
D, H, PAY = 1024, 384, 1152
TOK, BLK, HALF = 2, 16, 8
SLICES = 4
EXPERTS = 32


def body(tokens_hbm, routing_hbm, combine_hbm, gate_hbm, up_hbm, down_hbm, out,
         tokens, routing, combine, gate, up, down, pay, rows1, stage, gath, part, rs, hid, perm,
         own, away, other, tmp, red, zf, zsend, zrecv,
         wsem, insem, s1, r1, s2, r2, s3, r3, s4, r4, s5, r5, s6, r6, s7, r7, s8, r8):
    me = lax.axis_index("expert")
    x = lax.axis_index("dp")
    c = lax.rem(me, 2)
    y = lax.rem(me // 2, LINE)
    z = me // (2 * LINE)
    e = me // SLICES
    partner = (me + 1 - 2 * c, x)

    def along_y(d):
        return ((z * LINE + lax.rem(y + d, LINE)) * 2 + c, x)

    def at_z(zz):
        return ((zz * LINE + y) * 2 + c, x)

    def over(d):
        return (me, lax.rem(x + d, 4))

    def copy(src, dst, ssem, rsem, to):
        return pltpu.make_async_remote_copy(
            src_ref=src, dst_ref=dst, send_sem=ssem, recv_sem=rsem, device_id=to, device_id_type=MESH)

    def send(*args):
        cp = copy(*args)
        cp.start()
        return cp

    def signal(sem, to):
        pl.semaphore_signal(sem, inc=1, device_id=to, device_id_type=MESH)

    barrier = pltpu.get_barrier_semaphore()
    for d in FAR:
        signal(barrier, along_y(d))
    for d in DP:
        signal(barrier, over(d))
    signal(barrier, partner)
    for zs in range(1, LINE):
        @pl.when(zs > z)
        def _():
            signal(barrier, at_z(zs))

    loads = [pltpu.make_async_copy(src, dst, wsem.at[i]) for i, (src, dst) in enumerate((
        (tokens_hbm, tokens), (routing_hbm, routing), (combine_hbm, combine),
        (gate_hbm, gate), (up_hbm, up), (down_hbm, down)))]
    for cp in loads:
        cp.start()
    for cp in loads[:3]:
        cp.wait()

    pay[:, :D] = tokens[...]
    lane = lax.broadcasted_iota(jnp.int32, (TOK, 128), 1)
    dense = jnp.zeros((TOK, 128), F32)
    for k in range(8):
        dense = dense + jnp.where(lax.rem(lane, EXPERTS) == routing[:, k:k + 1], combine[:, k:k + 1], 0.0)
    high = dense.astype(BF16).astype(F32)
    pay[:, D:] = jnp.where(lane < EXPERTS, high, jnp.where(lane < 2 * EXPERTS, dense - high, 0.0)).astype(BF16)
    pl.semaphore_wait(barrier, 11 + z)
    for zs in range(LINE - 1):
        @pl.when(zs < z)
        def _():
            signal(insem.at[z], at_z(zs))

    c1 = {d: send(pay, rows1.at[d], s1.at[d], r1.at[d], along_y(d)) for d in FAR}
    stage[0:TOK, :] = pay[...].astype(F32)

    r = lax.broadcasted_iota(jnp.int32, (128, 128), 0)
    k = lax.broadcasted_iota(jnp.int32, (128, 128), 1)
    core = lax.rem(r // 64 + c, 2)
    source = lax.rem(r // 2, 4) * 32 + core * 16 + lax.rem(r // 8, 8) * 2 + lax.rem(r, 2)
    perm[...] = jnp.where(k == source, 1.0, 0.0).astype(BF16)

    for d in NEAR:
        c1[d].wait_recv()
        stage[TOK * d:TOK * d + TOK, :] = rows1[d].astype(F32)
    gath[z, c] = stage[...].astype(BF16)

    mine = gath.at[z, c]
    send(mine, mine, s3.at[z], r3.at[z], partner)
    for zs in range(LINE):
        @pl.when(zs > z)
        def _():
            pl.semaphore_wait(insem.at[zs], 1)

        @pl.when(zs != z)
        def _():
            send(mine, mine, s2.at[zs], r2.at[z], at_z(zs))

    def block(zs):
        return copy(gath.at[zs, c], gath.at[zs, c], s2.at[zs], r2.at[zs], partner)

    def onward(zs):
        return copy(gath.at[zs, c], gath.at[zs, c], s3.at[zs], r3.at[zs], partner)

    def take(g):
        for zs in range(4 * g, 4 * g + 4):
            @pl.when(zs != z)
            def _():
                block(zs).wait_recv()
                onward(zs).start()

    def meet(g):
        for zs in range(4 * g, 4 * g + 4):
            copy(gath.at[zs, 1 - c], gath.at[zs, 1 - c], s3.at[zs], r3.at[zs], partner).wait_recv()

    def linear(g):
        rows = gath[4 * g:4 * g + 4, :, :, :D].reshape(128, D)
        for i, w in enumerate((gate, up)):
            lin = lax.dot_general(rows, w[...], (((1,), (1,)), ((), ())), preferred_element_type=F32)
            part[g, :, :, i * H:(i + 1) * H] = lin.astype(BF16).reshape(4, 32, H)
        return {d: send(part.at[g, lax.rem(x + d, 4)], rs.at[g, d], s4.at[g, d], r4.at[g, d], over(d)) for d in DP}

    lanes = lax.broadcasted_iota(jnp.int32, (32, 128), 1)
    named = (lanes == e) | (lanes == e + EXPERTS)

    def activate(g, c4):
        total = part[g, x].astype(F32)
        for d in (1, 3, 2):
            c4[d].wait_recv()
            total = total + rs[g, d].astype(F32)
        wrow = gath[4 * g + x, :, :, D:].reshape(32, 128).astype(F32)
        weight = jnp.sum(jnp.where(named, wrow, 0.0), axis=1, keepdims=True)
        gt, u = total[:, :H], total[:, H:]
        hid[g, x] = (jax.nn.sigmoid(gt) * gt * u * weight).astype(BF16)
        return {d: send(hid.at[g, x], hid.at[g, x], s5.at[g, d], r5.at[g, d], over(d)) for d in DP}

    def arrived(g):
        for d in (1, 3, 2):
            src = lax.rem(x + 4 - d, 4)
            copy(hid.at[g, src], hid.at[g, src], s5.at[g, d], r5.at[g, d], over(d)).wait_recv()

    def product(g):
        arrived(g)
        h = jnp.dot(perm[...], hid[g].reshape(128, H), preferred_element_type=F32).astype(BF16)
        away[g] = jnp.dot(h[64:], down[...], preferred_element_type=F32).astype(BF16).reshape(LINE, HALF, D)
        cp = send(away.at[g], other.at[g], s6.at[g], r6.at[g], partner)
        own[g] = jnp.dot(h[:64], down[...], preferred_element_type=F32).reshape(LINE, HALF, D)
        return cp

    def cores(g, c6):
        c6.wait_recv()
        c7 = {}
        for d in FAR:
            tmp[g, d] = (own[g, d] + other[g, d].astype(F32)).astype(BF16)
            c7[d] = send(tmp.at[g, d], red.at[g, d], s7.at[g, d], r7.at[g, d], along_y(LINE - d))
        own[g, 0] = own[g, 0] + other[g, 0].astype(F32)
        return c7

    def line(g, c7):
        total = own[g, 0]
        for d in NEAR:
            c7[d].wait_recv()
            total = total + red[g, d].astype(F32)
        own[g, 0] = total
        for q in range(4):
            piece = own[g, 0, TOK * q:TOK * q + TOK, :]
            zf[4 * g + q] = piece
            zsend[4 * g + q] = piece.astype(BF16)

            @pl.when(4 * g + q != z)
            def _():
                send(zsend.at[4 * g + q], zrecv.at[z], s8.at[4 * g + q], r8.at[z], at_z(4 * g + q))

    take(0)
    for cp in loads[3:]:
        cp.wait()
    meet(0)
    c40 = linear(0)
    take(1)
    c50 = activate(0, c40)
    meet(1)
    c41 = linear(1)
    c60 = product(0)
    c51 = activate(1, c41)
    c70 = cores(0, c60)
    c61 = product(1)
    line(0, c70)
    c71 = cores(1, c61)
    line(1, c71)

    final = zf[z]
    for d in NEAR:
        src = lax.rem(z + d, LINE)
        copy(zsend.at[src], zrecv.at[src], s8.at[src], r8.at[src], partner).wait_recv()
        final = final + zrecv[src].astype(F32)
    out[...] = final.astype(BF16)

    for group in (c1, c40, c41, c50, c51, c70, c71):
        for cp in group.values():
            cp.wait_send()
    c60.wait_send()
    c61.wait_send()
    for zs in range(LINE):
        onward(zs).wait_send()

        @pl.when(zs != z)
        def _():
            block(zs).wait_send()
            copy(zsend.at[zs], zrecv.at[zs], s8.at[zs], r8.at[zs], partner).wait_send()


def shards(tokens, routing, combine, gate, up, down):
    hbm = pl.BlockSpec(memory_space=pl.ANY)
    dma = pltpu.SemaphoreType.DMA
    return pl.pallas_call(
        body,
        out_shape=jax.ShapeDtypeStruct((TOK, D), BF16),
        in_specs=[hbm] * 6,
        out_specs=pl.BlockSpec(memory_space=pltpu.VMEM),
        scratch_shapes=[
            pltpu.VMEM((TOK, D), BF16), pltpu.VMEM((TOK, 8), jnp.int32), pltpu.VMEM((TOK, 8), F32),
            pltpu.VMEM((H, D), BF16), pltpu.VMEM((H, D), BF16), pltpu.VMEM((H, D), BF16),
            pltpu.VMEM((TOK, PAY), BF16),
            pltpu.VMEM((LINE, TOK, PAY), BF16),
            pltpu.VMEM((BLK, PAY), F32),
            pltpu.VMEM((LINE, 2, BLK, PAY), BF16),
            pltpu.VMEM((2, 4, 32, 2 * H), BF16),
            pltpu.VMEM((2, 4, 32, 2 * H), BF16),
            pltpu.VMEM((2, 4, 32, H), BF16),
            pltpu.VMEM((128, 128), BF16),
            pltpu.VMEM((2, LINE, HALF, D), F32),
            pltpu.VMEM((2, LINE, HALF, D), BF16),
            pltpu.VMEM((2, LINE, HALF, D), BF16),
            pltpu.VMEM((2, LINE, HALF, D), BF16),
            pltpu.VMEM((2, LINE, HALF, D), BF16),
            pltpu.VMEM((LINE, TOK, D), F32),
            pltpu.VMEM((LINE, TOK, D), BF16),
            pltpu.VMEM((LINE, TOK, D), BF16),
            dma((6,)), pltpu.SemaphoreType.REGULAR((8,)),
            dma((8,)), dma((8,)), dma((8,)), dma((8,)), dma((8,)), dma((8,)),
            dma((2, 4)), dma((2, 4)), dma((2, 4)), dma((2, 4)),
            dma((2,)), dma((2,)), dma((2, 8)), dma((2, 8)), dma((8,)), dma((8,)),
        ],
        compiler_params=pltpu.CompilerParams(
            collective_id=0, has_side_effects=True, vmem_limit_bytes=60 << 20),
        cost_estimate=pl.CostEstimate(flops=603979776, bytes_accessed=2400000, transcendentals=24576),
    )(tokens, routing, combine, gate, up, down)


def solution(mesh):
    return jax.shard_map(
        shards,
        mesh=mesh,
        in_specs=(
            P("expert", "dp"),
            P("expert", None),
            P("expert", None),
            P("expert", "dp"),
            P("expert", "dp"),
            P("expert", "dp"),
        ),
        out_specs=P("expert", "dp"),
        check_vma=False,
    )
```

```python
import jax
import jax.numpy as jnp
from jax import lax
from jax.experimental import pallas as pl
from jax.experimental.pallas import tpu as pltpu
from jax.sharding import PartitionSpec as P

MESH = pl.DeviceIdType.MESH
F32, BF16 = jnp.float32, jnp.bfloat16
LINE = 8
FAR = (4, 3, 5, 2, 6, 1, 7)
NEAR = (1, 7, 2, 6, 3, 5, 4)
EARLY = (0, 1, 2, 3, 7, 6, 5, 4)
D, H, PAY = 1024, 384, 1152
TOK, BLK = 2, 16
GROUPS = 4
DEEP = LINE // GROUPS
ROWS = DEEP * 2 * BLK
PART = ROWS // 4
PIECE = DEEP * TOK
EARLIER = 3
MID = EARLIER * DEEP
SLICES = 4
EXPERTS = 32


def body(tokens_hbm, routing_hbm, combine_hbm, gate_hbm, up_hbm, down_hbm, out,
         tokens, routing, combine, gate, up, turned, down, pay, rows1, stage, gath, part, rs, hid, perm,
         perm2, own, away, other, tmp, red, zf, zsend, zrecv,
         own2, away2, other2, tmp2, red2, sum2, ysend, yrecv,
         wsem, inz, iny, inx, inc, s1, r1, s2, r2, s3, r3, s4, r4, s5, r5, s6, r6, s7, r7, s8, r8, s9, r9, s10, r10):
    me = lax.axis_index("expert")
    x = lax.axis_index("dp")
    c = lax.rem(me, 2)
    y = lax.rem(me // 2, LINE)
    z = me // (2 * LINE)
    e = me // SLICES
    partner = (me + 1 - 2 * c, x)

    def at_y(yy):
        return ((z * LINE + yy) * 2 + c, x)

    def along_y(d):
        return at_y(lax.rem(y + d, LINE))

    def at_z(zz):
        return ((zz * LINE + y) * 2 + c, x)

    def copy(src, dst, ssem, rsem, to):
        return pltpu.make_async_remote_copy(
            src_ref=src, dst_ref=dst, send_sem=ssem, recv_sem=rsem, device_id=to, device_id_type=MESH)

    def send(*args):
        cp = copy(*args)
        cp.start()
        return cp

    def signal(sem, to):
        pl.semaphore_signal(sem, inc=1, device_id=to, device_id_type=MESH)

    barrier = pltpu.get_barrier_semaphore()
    rank = y + (y // 4) * (11 - 2 * y)

    def later(act):
        for zs in range(1, LINE):
            @pl.when(zs > z)
            def _():
                act(at_z(zs))
        for i, ys in enumerate(EARLY):
            @pl.when(i > rank)
            def _():
                act(at_y(ys))
        for xs in range(1, 4):
            @pl.when(xs > x)
            def _():
                act((me, xs))

        @pl.when(c == 1)
        def _():
            act(partner)

    later(lambda to: signal(barrier, to))
    loads = [pltpu.make_async_copy(src, dst, wsem.at[i]) for i, (src, dst) in enumerate((
        (tokens_hbm, tokens), (routing_hbm, routing), (combine_hbm, combine),
        (gate_hbm, gate), (up_hbm, up), (down_hbm, down)))]
    for cp in loads:
        cp.start()
    for cp in loads[:3]:
        cp.wait()
    pay[:, :D] = tokens[...]
    lane = lax.broadcasted_iota(jnp.int32, (TOK, 128), 1)
    number = jnp.where(lane < EXPERTS, lane, lane - EXPERTS)
    dense = jnp.zeros((TOK, 128), F32)
    for k in range(8):
        dense = dense + jnp.where(number == routing[:, k:k + 1], combine[:, k:k + 1], 0.0)
    high = dense.astype(BF16).astype(F32)
    pay[:, D:] = jnp.where(lane < EXPERTS, high, jnp.where(lane < 2 * EXPERTS, dense - high, 0.0)).astype(BF16)

    before = z + rank + x + 1 - c

    @pl.when(before > 0)
    def _():
        pl.semaphore_wait(barrier, before)

    for zs in range(LINE - 1):
        @pl.when(zs < z)
        def _():
            signal(inz.at[z], at_z(zs))
    for i, ys in enumerate(EARLY):
        @pl.when(i < rank)
        def _():
            signal(iny.at[y], at_y(ys))
    for xs in range(3):
        @pl.when(xs < x)
        def _():
            signal(inx.at[x], (me, xs))

    @pl.when(c == 0)
    def _():
        signal(inc, partner)

    for i, ys in enumerate(EARLY):
        @pl.when(i > rank)
        def _():
            pl.semaphore_wait(iny.at[ys], 1)

        @pl.when(i != rank)
        def _():
            d = lax.rem(ys - y + LINE, LINE)
            send(pay, rows1.at[d], s1.at[d], r1.at[d], at_y(ys))
    stage[0:TOK, :] = pay[...].astype(F32)

    def greeting(d):
        return copy(pay, rows1.at[d], s1.at[d], r1.at[d], partner)

    r = lax.broadcasted_iota(jnp.int32, (ROWS, ROWS), 0)
    k = lax.broadcasted_iota(jnp.int32, (ROWS, ROWS), 1)
    core = (r // (ROWS // 2) + c) & 1
    place = (r // PIECE) & 7
    dist = 4 + ((place + 1) // 2) * (1 - 2 * (place & 1))
    source = ((r // 2) & (DEEP - 1)) * 32 + core * 16 + dist * 2 + (r & 1)
    perm[...] = jnp.where(k == source, 1.0, 0.0).astype(BF16)
    source = ((r // BLK) & (DEEP - 1)) * 32 + core * 16 + (r & 15)
    perm2[...] = jnp.where(k == source, 1.0, 0.0).astype(BF16)

    for cp in loads[3:]:
        cp.wait()
    turned[:, :H] = gate[...].T
    turned[:, H:] = up[...].T
    for d in NEAR:
        greeting(d).wait_recv()
        stage[TOK * d:TOK * d + TOK, :] = rows1[d].astype(F32)
    gath[z, c] = stage[...].astype(BF16)

    mine = gath.at[z, c]

    @pl.when(c == 1)
    def _():
        pl.semaphore_wait(inc, 1)

    send(mine, mine, s3.at[z], r3.at[z], partner)
    for zs in range(LINE):
        @pl.when(zs > z)
        def _():
            pl.semaphore_wait(inz.at[zs], 1)

        @pl.when(zs != z)
        def _():
            send(mine, mine, s2.at[zs], r2.at[z], at_z(zs))

    def block(zs):
        return copy(gath.at[zs, c], gath.at[zs, c], s2.at[zs], r2.at[zs], partner)

    def onward(zs):
        return copy(gath.at[zs, c], gath.at[zs, c], s3.at[zs], r3.at[zs], partner)

    def take(g):
        for zs in range(DEEP * g, DEEP * g + DEEP):
            @pl.when(zs != z)
            def _():
                block(zs).wait_recv()
                onward(zs).start()

    def meet(zs):
        copy(gath.at[zs, 1 - c], gath.at[zs, 1 - c], s3.at[zs], r3.at[zs], partner).wait_recv()

    def share(g, xs):
        return copy(part.at[g, xs], rs.at[g, x], s4.at[g, xs], r4.at[g, x], (me, xs))

    def linear(g):
        for zs in range(DEEP * g, DEEP * g + DEEP):
            meet(zs)
        rows = gath[DEEP * g:DEEP * g + DEEP, :, :, :D].reshape(ROWS, D)
        lin = jnp.dot(rows, turned[...], preferred_element_type=F32)
        part[g] = lin.astype(BF16).reshape(4, PART, 2 * H)
        for xs in range(4):
            if g == 0:
                @pl.when(xs > x)
                def _():
                    pl.semaphore_wait(inx.at[xs], 1)

            @pl.when(xs != x)
            def _():
                share(g, xs).start()

    lanes = lax.broadcasted_iota(jnp.int32, (PART, 128), 1)
    named = (lanes == e) | (lanes == e + EXPERTS)

    def spread(g, d):
        to = (me, lax.rem(x + d, 4))
        return copy(hid.at[g, x], hid.at[g, x], s5.at[g, d], r5.at[g, d], to)

    def activate(g):
        total = part[g, x].astype(F32)
        for d in (1, 3, 2):
            xs = lax.rem(x + d, 4)
            copy(part.at[g, xs], rs.at[g, xs], s4.at[g, xs], r4.at[g, xs], (me, xs)).wait_recv()
            total = total + rs[g, xs].astype(F32)
        wrow = gath[DEEP * g + x // 2, lax.rem(x, 2), :, D:].astype(F32)
        weight = jnp.sum(jnp.where(named, wrow, 0.0), axis=1, keepdims=True)
        gt, u = total[:, :H], total[:, H:]
        hid[g, x] = (jax.nn.sigmoid(gt) * gt * u * weight).astype(BF16)
        for d in (2, 1, 3):
            spread(g, d).start()

    def product(g):
        for d in (1, 3, 2):
            src = lax.rem(x + 4 - d, 4)
            copy(hid.at[g, src], hid.at[g, src], s5.at[g, d], r5.at[g, d], partner).wait_recv()
        early, i = g < EARLIER, g % EARLIER
        order, mine_ref, to, at, shape = (
            (perm, own, away, other, (LINE, PIECE, D)) if early else (perm2, own2, away2, other2, (DEEP, BLK, D)))
        h = jnp.dot(order[...], hid[g].reshape(ROWS, H), preferred_element_type=F32).astype(BF16)
        both = jnp.dot(h, down[...], preferred_element_type=F32)
        to[i] = both[ROWS // 2:].astype(BF16).reshape(shape)
        cp = send(to.at[i], at.at[i], s6.at[g], r6.at[g], partner)
        mine_ref[i] = both[:ROWS // 2].reshape(shape)
        return cp

    def back(zs):
        i, q = (zs - MID) // DEEP, (zs - MID) % DEEP
        return copy(tmp2.at[i, q], red2.at[z], s9.at[zs], r9.at[z], at_z(zs))

    def cores2(g, c6):
        i = g - EARLIER
        c6.wait_recv()
        for q in range(DEEP):
            zs = DEEP * g + q
            both = own2[i, q] + other2[i, q].astype(F32)
            tmp2[i, q] = both.astype(BF16)

            @pl.when(zs != z)
            def _():
                back(zs).start()

            @pl.when(zs == z)
            def _():
                sum2[...] = both

    def cores(g, c6):
        c6.wait_recv()
        c7 = {}
        for i, d in enumerate(FAR + (0,)):
            both = own[g, i] + other[g, i].astype(F32)
            if d:
                tmp[g, i] = both.astype(BF16)
                c7[d] = send(tmp.at[g, i], red.at[g, d], s7.at[g, d], r7.at[g, d], along_y(LINE - d))
            else:
                own[g, 0] = both
        return c7

    def line(g, c7):
        total = own[g, 0]
        for d in NEAR:
            c7[d].wait_recv()
            total = total + red[g, d].astype(F32)
        own[g, 0] = total
        for q in range(DEEP):
            piece = own[g, 0, TOK * q:TOK * q + TOK, :]
            zf[DEEP * g + q] = piece
            zsend[DEEP * g + q] = piece.astype(BF16)

            @pl.when(DEEP * g + q != z)
            def _():
                send(zsend.at[DEEP * g + q], zrecv.at[z], s8.at[DEEP * g + q], r8.at[z], at_z(DEEP * g + q))

    c6, c7 = {}, {}
    take(0)
    linear(0)
    take(1)
    linear(1)
    activate(0)
    take(2)
    take(3)
    linear(2)
    c6[0] = product(0)
    activate(1)
    linear(3)
    c7[0] = cores(0, c6[0])
    activate(2)
    c6[1] = product(1)
    activate(3)
    c7[1] = cores(1, c6[1])
    c6[2] = product(2)
    line(0, c7[0])
    c7[2] = cores(2, c6[2])
    c6[3] = product(3)
    cores2(3, c6[3])
    line(1, c7[1])
    line(2, c7[2])

    @pl.when(z < MID)
    def _():
        final = zf[z]
        for d in NEAR:
            src = lax.rem(z + d, LINE)
            copy(zsend.at[0], zrecv.at[src], s8.at[0], r8.at[src], partner).wait_recv()
            final = final + zrecv[src].astype(F32)
        out[...] = final.astype(BF16)

    def row(d):
        return copy(ysend.at[d], yrecv.at[d], s10.at[d], r10.at[d], along_y(LINE - d))

    @pl.when(z >= MID)
    def _():
        total = sum2[...]
        for d in NEAR:
            src = lax.rem(z + d, LINE)
            copy(tmp2.at[0, 0], red2.at[src], s9.at[src], r9.at[src], partner).wait_recv()
            total = total + red2[src].astype(F32)
        sum2[...] = total
        for d in FAR:
            ysend[d] = sum2[TOK * d:TOK * d + TOK, :].astype(BF16)
            row(d).start()
        final = sum2[0:TOK, :]
        for d in NEAR:
            row(d).wait_recv()
            final = final + yrecv[d].astype(F32)
        out[...] = final.astype(BF16)
        for d in NEAR:
            row(d).wait_send()

    for g in range(GROUPS):
        c6[g].wait_send()
        for cp in c7[g].values() if g in c7 else ():
            cp.wait_send()
        for d in (1, 2, 3):
            spread(g, d).wait_send()
        for xs in range(4):
            @pl.when(xs != x)
            def _():
                share(g, xs).wait_send()
    for d in NEAR:
        greeting(d).wait_send()
    for zs in range(LINE):
        onward(zs).wait_send()

        @pl.when(zs != z)
        def _():
            block(zs).wait_send()
            if zs < MID:
                copy(zsend.at[zs], zrecv.at[z], s8.at[zs], r8.at[z], partner).wait_send()
            else:
                back(zs).wait_send()


def shards(tokens, routing, combine, gate, up, down):
    hbm = pl.BlockSpec(memory_space=pl.ANY)
    dma, flag = pltpu.SemaphoreType.DMA, pltpu.SemaphoreType.REGULAR
    return pl.pallas_call(
        body,
        out_shape=jax.ShapeDtypeStruct((TOK, D), BF16),
        in_specs=[hbm] * 6,
        out_specs=pl.BlockSpec(memory_space=pltpu.VMEM),
        scratch_shapes=[
            pltpu.VMEM((TOK, D), BF16), pltpu.VMEM((TOK, 8), jnp.int32), pltpu.VMEM((TOK, 8), F32),
            pltpu.VMEM((H, D), BF16), pltpu.VMEM((H, D), BF16), pltpu.VMEM((D, 2 * H), BF16), pltpu.VMEM((H, D), BF16),
            pltpu.VMEM((TOK, PAY), BF16),
            pltpu.VMEM((LINE, TOK, PAY), BF16),
            pltpu.VMEM((BLK, PAY), F32),
            pltpu.VMEM((LINE, 2, BLK, PAY), BF16),
            pltpu.VMEM((GROUPS, 4, PART, 2 * H), BF16),
            pltpu.VMEM((GROUPS, 4, PART, 2 * H), BF16),
            pltpu.VMEM((GROUPS, 4, PART, H), BF16),
            pltpu.VMEM((ROWS, ROWS), BF16), pltpu.VMEM((ROWS, ROWS), BF16),
            pltpu.VMEM((EARLIER, LINE, PIECE, D), F32),
            pltpu.VMEM((EARLIER, LINE, PIECE, D), BF16),
            pltpu.VMEM((EARLIER, LINE, PIECE, D), BF16),
            pltpu.VMEM((EARLIER, LINE, PIECE, D), BF16),
            pltpu.VMEM((EARLIER, LINE, PIECE, D), BF16),
            pltpu.VMEM((MID, TOK, D), F32),
            pltpu.VMEM((MID, TOK, D), BF16),
            pltpu.VMEM((LINE, TOK, D), BF16),
            pltpu.VMEM((EARLIER, DEEP, BLK, D), F32),
            pltpu.VMEM((EARLIER, DEEP, BLK, D), BF16),
            pltpu.VMEM((EARLIER, DEEP, BLK, D), BF16),
            pltpu.VMEM((EARLIER, DEEP, BLK, D), BF16),
            pltpu.VMEM((LINE, BLK, D), BF16),
            pltpu.VMEM((BLK, D), F32),
            pltpu.VMEM((LINE, TOK, D), BF16),
            pltpu.VMEM((LINE, TOK, D), BF16),
            dma((6,)), flag((8,)), flag((8,)), flag((4,)), flag,
            dma((8,)), dma((8,)), dma((8,)), dma((8,)), dma((8,)), dma((8,)),
            dma((GROUPS, 4)), dma((GROUPS, 4)), dma((GROUPS, 4)), dma((GROUPS, 4)),
            dma((GROUPS,)), dma((GROUPS,)), dma((GROUPS, 8)), dma((GROUPS, 8)), dma((8,)), dma((8,)),
            dma((8,)), dma((8,)), dma((8,)), dma((8,)),
        ],
        compiler_params=pltpu.CompilerParams(
            collective_id=0, has_side_effects=True, vmem_limit_bytes=60 << 20),
        cost_estimate=pl.CostEstimate(flops=603979776, bytes_accessed=2400000, transcendentals=24576),
    )(tokens, routing, combine, gate, up, down)


def solution(mesh):
    return jax.shard_map(
        shards,
        mesh=mesh,
        in_specs=(
            P("expert", "dp"),
            P("expert", None),
            P("expert", None),
            P("expert", "dp"),
            P("expert", "dp"),
            P("expert", "dp"),
        ),
        out_specs=P("expert", "dp"),
        check_vma=False,
    )
```

```python
import jax
import jax.numpy as jnp
from jax import lax
from jax.experimental import pallas as pl
from jax.experimental.pallas import tpu as pltpu
from jax.sharding import PartitionSpec as P

MESH = pl.DeviceIdType.MESH
F32, BF16 = jnp.float32, jnp.bfloat16
LINE = 8
FAR = (4, 3, 5, 2, 6, 1, 7)
NEAR = (1, 7, 2, 6, 3, 5, 4)
EARLY = (0, 1, 2, 3, 7, 6, 5, 4)
D, H, PAY = 1024, 384, 1152
TOK, BLK = 2, 16
GROUPS = 4
DEEP = LINE // GROUPS
ROWS = DEEP * 2 * BLK
PART = ROWS // 4
PIECE = DEEP * TOK
EARLIER = 3
MID = EARLIER * DEEP
SLICES = 4
EXPERTS = 32


def body(tokens_hbm, routing_hbm, combine_hbm, gate_hbm, up_hbm, down_hbm, out,
         tokens, routing, combine, gate, up, turned, down, pay, rows1, stage, gath, part, rs, hid, perm,
         perm2, own, away, other, tmp, red, zf, zsend, zrecv,
         own2, away2, other2, tmp2, red2, sum2, ysend, yrecv,
         wsem, inz, iny, inx, inc, s1, r1, s2, r2, s3, r3, s4, r4, s5, r5, s6, r6, s7, r7, s8, r8, s9, r9, s10, r10):
    me = lax.axis_index("expert")
    x = lax.axis_index("dp")
    c = lax.rem(me, 2)
    y = lax.rem(me // 2, LINE)
    z = me // (2 * LINE)
    e = me // SLICES
    partner = (me + 1 - 2 * c, x)

    def at_y(yy):
        return ((z * LINE + yy) * 2 + c, x)

    def along_y(d):
        return at_y(lax.rem(y + d, LINE))

    def at_z(zz):
        return ((zz * LINE + y) * 2 + c, x)

    def copy(src, dst, ssem, rsem, to):
        return pltpu.make_async_remote_copy(
            src_ref=src, dst_ref=dst, send_sem=ssem, recv_sem=rsem, device_id=to, device_id_type=MESH)

    def send(*args):
        cp = copy(*args)
        cp.start()
        return cp

    def signal(sem, to):
        pl.semaphore_signal(sem, inc=1, device_id=to, device_id_type=MESH)

    barrier = pltpu.get_barrier_semaphore()
    rank = y + (y // 4) * (11 - 2 * y)

    def later(act):
        for zs in range(1, LINE):
            @pl.when(zs > z)
            def _():
                act(at_z(zs))
        for i, ys in enumerate(EARLY):
            @pl.when(i > rank)
            def _():
                act(at_y(ys))
        for xs in range(1, 4):
            @pl.when(xs > x)
            def _():
                act((me, xs))

        @pl.when(c == 1)
        def _():
            act(partner)

    later(lambda to: signal(barrier, to))
    loads = [pltpu.make_async_copy(src, dst, wsem.at[i]) for i, (src, dst) in enumerate((
        (tokens_hbm, tokens), (routing_hbm, routing), (combine_hbm, combine),
        (gate_hbm, gate), (up_hbm, up), (down_hbm, down)))]
    for cp in loads:
        cp.start()
    for cp in loads[:3]:
        cp.wait()
    pay[:, :D] = tokens[...]
    lane = lax.broadcasted_iota(jnp.int32, (TOK, 128), 1)
    number = jnp.where(lane < EXPERTS, lane, lane - EXPERTS)
    dense = jnp.zeros((TOK, 128), F32)
    for k in range(8):
        dense = dense + jnp.where(number == routing[:, k:k + 1], combine[:, k:k + 1], 0.0)
    high = dense.astype(BF16).astype(F32)
    pay[:, D:] = jnp.where(lane < EXPERTS, high, jnp.where(lane < 2 * EXPERTS, dense - high, 0.0)).astype(BF16)

    before = z + rank + x + 1 - c

    @pl.when(before > 0)
    def _():
        pl.semaphore_wait(barrier, before)

    for zs in range(LINE - 1):
        @pl.when(zs < z)
        def _():
            signal(inz.at[z], at_z(zs))
    for i, ys in enumerate(EARLY):
        @pl.when(i < rank)
        def _():
            signal(iny.at[y], at_y(ys))
    for xs in range(3):
        @pl.when(xs < x)
        def _():
            signal(inx.at[x], (me, xs))

    @pl.when(c == 0)
    def _():
        signal(inc, partner)

    for i, ys in enumerate(EARLY):
        @pl.when(i > rank)
        def _():
            pl.semaphore_wait(iny.at[ys], 1)

        @pl.when(i != rank)
        def _():
            d = lax.rem(ys - y + LINE, LINE)
            send(pay, rows1.at[d], s1.at[d], r1.at[d], at_y(ys))
    stage[0:TOK, :] = pay[...].astype(F32)

    def greeting(d):
        return copy(pay, rows1.at[d], s1.at[d], r1.at[d], partner)

    r = lax.broadcasted_iota(jnp.int32, (ROWS, ROWS), 0)
    k = lax.broadcasted_iota(jnp.int32, (ROWS, ROWS), 1)
    core = (r // (ROWS // 2) + c) & 1
    place = (r // PIECE) & 7
    dist = 4 + ((place + 1) // 2) * (1 - 2 * (place & 1))
    source = ((r // 2) & (DEEP - 1)) * 32 + core * 16 + dist * 2 + (r & 1)
    perm[...] = jnp.where(k == source, 1.0, 0.0).astype(BF16)
    source = ((r // BLK) & (DEEP - 1)) * 32 + core * 16 + (r & 15)
    perm2[...] = jnp.where(k == source, 1.0, 0.0).astype(BF16)

    for cp in loads[3:]:
        cp.wait()
    turned[:, :H] = gate[...].T
    turned[:, H:] = up[...].T
    for d in NEAR:
        greeting(d).wait_recv()
        stage[TOK * d:TOK * d + TOK, :] = rows1[d].astype(F32)
    gath[z, c] = stage[...].astype(BF16)

    mine = gath.at[z, c]

    @pl.when(c == 1)
    def _():
        pl.semaphore_wait(inc, 1)

    send(mine, mine, s3.at[z], r3.at[z], partner)
    for zs in range(LINE):
        @pl.when(zs > z)
        def _():
            pl.semaphore_wait(inz.at[zs], 1)

        @pl.when(zs != z)
        def _():
            send(mine, mine, s2.at[zs], r2.at[z], at_z(zs))

    def block(zs):
        return copy(gath.at[zs, c], gath.at[zs, c], s2.at[zs], r2.at[zs], partner)

    def onward(zs):
        return copy(gath.at[zs, c], gath.at[zs, c], s3.at[zs], r3.at[zs], partner)

    def take(g):
        for zs in range(DEEP * g, DEEP * g + DEEP):
            @pl.when(zs != z)
            def _():
                block(zs).wait_recv()
                onward(zs).start()

    def meet(zs):
        copy(gath.at[zs, 1 - c], gath.at[zs, 1 - c], s3.at[zs], r3.at[zs], partner).wait_recv()

    def share(g, xs):
        return copy(part.at[g, xs], rs.at[g, x], s4.at[g, xs], r4.at[g, x], (me, xs))

    def linear(g):
        for zs in range(DEEP * g, DEEP * g + DEEP):
            meet(zs)
        rows = gath[DEEP * g:DEEP * g + DEEP, :, :, :D].reshape(ROWS, D)
        lin = jnp.dot(rows, turned[...], preferred_element_type=F32)
        part[g] = lin.astype(BF16).reshape(4, PART, 2 * H)
        for d in (2, 1, 3):
            xs = lax.rem(x + d, 4)
            if g == 0:
                @pl.when(xs > x)
                def _():
                    pl.semaphore_wait(inx.at[xs], 1)

            share(g, xs).start()

    lanes = lax.broadcasted_iota(jnp.int32, (PART, 128), 1)
    named = (lanes == e) | (lanes == e + EXPERTS)

    def spread(g, d):
        to = (me, lax.rem(x + d, 4))
        return copy(hid.at[g, x], hid.at[g, x], s5.at[g, d], r5.at[g, d], to)

    def activate(g):
        total = part[g, x].astype(F32)
        for d in (1, 3, 2):
            xs = lax.rem(x + d, 4)
            copy(part.at[g, xs], rs.at[g, xs], s4.at[g, xs], r4.at[g, xs], (me, xs)).wait_recv()
            total = total + rs[g, xs].astype(F32)
        wrow = gath[DEEP * g + x // 2, lax.rem(x, 2), :, D:].astype(F32)
        weight = jnp.sum(jnp.where(named, wrow, 0.0), axis=1, keepdims=True)
        gt, u = total[:, :H], total[:, H:]
        hid[g, x] = (jax.nn.sigmoid(gt) * gt * u * weight).astype(BF16)
        for d in (2, 1, 3):
            spread(g, d).start()

    def product(g):
        for d in (1, 3, 2):
            src = lax.rem(x + 4 - d, 4)
            copy(hid.at[g, src], hid.at[g, src], s5.at[g, d], r5.at[g, d], partner).wait_recv()
        early, i = g < EARLIER, g % EARLIER
        order, mine_ref, to, at, shape = (
            (perm, own, away, other, (LINE, PIECE, D)) if early else (perm2, own2, away2, other2, (DEEP, BLK, D)))
        h = jnp.dot(order[...], hid[g].reshape(ROWS, H), preferred_element_type=F32).astype(BF16)
        both = jnp.dot(h, down[...], preferred_element_type=F32)
        to[i] = both[ROWS // 2:].astype(BF16).reshape(shape)
        cp = send(to.at[i], at.at[i], s6.at[g], r6.at[g], partner)
        mine_ref[i] = both[:ROWS // 2].reshape(shape)
        return cp

    def back(zs):
        i, q = (zs - MID) // DEEP, (zs - MID) % DEEP
        return copy(tmp2.at[i, q], red2.at[z], s9.at[zs], r9.at[z], at_z(zs))

    def cores2(g, c6):
        i = g - EARLIER
        c6.wait_recv()
        for q in range(DEEP):
            zs = DEEP * g + q
            both = own2[i, q] + other2[i, q].astype(F32)
            tmp2[i, q] = both.astype(BF16)

            @pl.when(zs != z)
            def _():
                back(zs).start()

            @pl.when(zs == z)
            def _():
                sum2[...] = both

    def cores(g, c6):
        c6.wait_recv()
        c7 = {}
        for i, d in enumerate(FAR + (0,)):
            both = own[g, i] + other[g, i].astype(F32)
            if d:
                tmp[g, i] = both.astype(BF16)
                c7[d] = send(tmp.at[g, i], red.at[g, d], s7.at[g, d], r7.at[g, d], along_y(LINE - d))
            else:
                own[g, 0] = both
        return c7

    def line(g, c7):
        total = own[g, 0]
        for d in NEAR:
            c7[d].wait_recv()
            total = total + red[g, d].astype(F32)
        own[g, 0] = total
        for q in range(DEEP):
            piece = own[g, 0, TOK * q:TOK * q + TOK, :]
            zf[DEEP * g + q] = piece
            zsend[DEEP * g + q] = piece.astype(BF16)

            @pl.when(DEEP * g + q != z)
            def _():
                send(zsend.at[DEEP * g + q], zrecv.at[z], s8.at[DEEP * g + q], r8.at[z], at_z(DEEP * g + q))

    c6, c7 = {}, {}
    take(0)
    linear(0)
    take(1)
    linear(1)
    activate(0)
    take(2)
    take(3)
    linear(2)
    c6[0] = product(0)
    activate(1)
    linear(3)
    c7[0] = cores(0, c6[0])
    activate(2)
    c6[1] = product(1)
    activate(3)
    c7[1] = cores(1, c6[1])
    c6[2] = product(2)
    c7[2] = cores(2, c6[2])
    c6[3] = product(3)
    line(0, c7[0])
    cores2(3, c6[3])
    line(1, c7[1])
    line(2, c7[2])

    @pl.when(z < MID)
    def _():
        final = zf[z]
        for d in NEAR:
            src = lax.rem(z + d, LINE)
            copy(zsend.at[0], zrecv.at[src], s8.at[0], r8.at[src], partner).wait_recv()
            final = final + zrecv[src].astype(F32)
        out[...] = final.astype(BF16)

    def row(d):
        return copy(ysend.at[d], yrecv.at[d], s10.at[d], r10.at[d], along_y(LINE - d))

    @pl.when(z >= MID)
    def _():
        total = sum2[...]
        for d in NEAR:
            src = lax.rem(z + d, LINE)
            copy(tmp2.at[0, 0], red2.at[src], s9.at[src], r9.at[src], partner).wait_recv()
            total = total + red2[src].astype(F32)
        sum2[...] = total
        for d in FAR:
            ysend[d] = sum2[TOK * d:TOK * d + TOK, :].astype(BF16)
            row(d).start()
        final = sum2[0:TOK, :]
        for d in NEAR:
            row(d).wait_recv()
            final = final + yrecv[d].astype(F32)
        out[...] = final.astype(BF16)
        for d in NEAR:
            row(d).wait_send()

    for g in range(GROUPS):
        c6[g].wait_send()
        for cp in c7[g].values() if g in c7 else ():
            cp.wait_send()
        for d in (1, 2, 3):
            spread(g, d).wait_send()
        for xs in range(4):
            @pl.when(xs != x)
            def _():
                share(g, xs).wait_send()
    for d in NEAR:
        greeting(d).wait_send()
    for zs in range(LINE):
        onward(zs).wait_send()

        @pl.when(zs != z)
        def _():
            block(zs).wait_send()
            if zs < MID:
                copy(zsend.at[zs], zrecv.at[z], s8.at[zs], r8.at[z], partner).wait_send()
            else:
                back(zs).wait_send()


def shards(tokens, routing, combine, gate, up, down):
    hbm = pl.BlockSpec(memory_space=pl.ANY)
    dma, flag = pltpu.SemaphoreType.DMA, pltpu.SemaphoreType.REGULAR
    return pl.pallas_call(
        body,
        out_shape=jax.ShapeDtypeStruct((TOK, D), BF16),
        in_specs=[hbm] * 6,
        out_specs=pl.BlockSpec(memory_space=pltpu.VMEM),
        scratch_shapes=[
            pltpu.VMEM((TOK, D), BF16), pltpu.VMEM((TOK, 8), jnp.int32), pltpu.VMEM((TOK, 8), F32),
            pltpu.VMEM((H, D), BF16), pltpu.VMEM((H, D), BF16), pltpu.VMEM((D, 2 * H), BF16), pltpu.VMEM((H, D), BF16),
            pltpu.VMEM((TOK, PAY), BF16),
            pltpu.VMEM((LINE, TOK, PAY), BF16),
            pltpu.VMEM((BLK, PAY), F32),
            pltpu.VMEM((LINE, 2, BLK, PAY), BF16),
            pltpu.VMEM((GROUPS, 4, PART, 2 * H), BF16),
            pltpu.VMEM((GROUPS, 4, PART, 2 * H), BF16),
            pltpu.VMEM((GROUPS, 4, PART, H), BF16),
            pltpu.VMEM((ROWS, ROWS), BF16), pltpu.VMEM((ROWS, ROWS), BF16),
            pltpu.VMEM((EARLIER, LINE, PIECE, D), F32),
            pltpu.VMEM((EARLIER, LINE, PIECE, D), BF16),
            pltpu.VMEM((EARLIER, LINE, PIECE, D), BF16),
            pltpu.VMEM((EARLIER, LINE, PIECE, D), BF16),
            pltpu.VMEM((EARLIER, LINE, PIECE, D), BF16),
            pltpu.VMEM((MID, TOK, D), F32),
            pltpu.VMEM((MID, TOK, D), BF16),
            pltpu.VMEM((LINE, TOK, D), BF16),
            pltpu.VMEM((EARLIER, DEEP, BLK, D), F32),
            pltpu.VMEM((EARLIER, DEEP, BLK, D), BF16),
            pltpu.VMEM((EARLIER, DEEP, BLK, D), BF16),
            pltpu.VMEM((EARLIER, DEEP, BLK, D), BF16),
            pltpu.VMEM((LINE, BLK, D), BF16),
            pltpu.VMEM((BLK, D), F32),
            pltpu.VMEM((LINE, TOK, D), BF16),
            pltpu.VMEM((LINE, TOK, D), BF16),
            dma((6,)), flag((8,)), flag((8,)), flag((4,)), flag,
            dma((8,)), dma((8,)), dma((8,)), dma((8,)), dma((8,)), dma((8,)),
            dma((GROUPS, 4)), dma((GROUPS, 4)), dma((GROUPS, 4)), dma((GROUPS, 4)),
            dma((GROUPS,)), dma((GROUPS,)), dma((GROUPS, 8)), dma((GROUPS, 8)), dma((8,)), dma((8,)),
            dma((8,)), dma((8,)), dma((8,)), dma((8,)),
        ],
        compiler_params=pltpu.CompilerParams(
            collective_id=0, has_side_effects=True, vmem_limit_bytes=60 << 20),
        cost_estimate=pl.CostEstimate(flops=603979776, bytes_accessed=2400000, transcendentals=24576),
    )(tokens, routing, combine, gate, up, down)


def solution(mesh):
    return jax.shard_map(
        shards,
        mesh=mesh,
        in_specs=(
            P("expert", "dp"),
            P("expert", None),
            P("expert", None),
            P("expert", "dp"),
            P("expert", "dp"),
            P("expert", "dp"),
        ),
        out_specs=P("expert", "dp"),
        check_vma=False,
    )
```
